32 devices in a mesh: seq: 16 (over z, y, core), tp: 2 (over x).
Axes of the slice: x: 2, y: 2, z: 4, core: 2. Of those that a mesh axis runs over, the one named last changes fastest.
Arguments:
- tokens: bfloat16 [4096, 4096], P('seq', 'tp'), may hold values from -6 to 6
- ln_gain: float32 [4096], replicated, may hold values from 0.1 to 1.9
- ln_bias: float32 [4096], replicated, may hold values from -3 to 3
- w_qkv: bfloat16 [4096, 16, 3, 128], P('seq', 'tp'), may hold values from -3 to 3
- w_out: bfloat16 [16, 128, 4096], P('tp', None, 'seq'), may hold values from -0.25 to 0.25
- layer_scale: float32 [4096], P('tp'), may hold values from 0.5 to 2
- grids: int32 [2], replicated, may hold values from 24 to 40, as said below
- offsets: int32 [3], replicated, may hold values from 0 to 2186, as said below
Outputs:
- merged: bfloat16 [4096, 4, 4096], P('seq', None, 'tp')
The draws below stay inside these ranges and needn't reach their ends.
Inputs may be any that keep to these rules, and one draw needn't show every extreme that they name: `grids`: every side is even and some image has side exactly 40. Of images 2k and 2k + 1, one side is drawn and the other is the largest even side of at most 40 whose square keeps the two squares' sum within 2176. offsets[0] = 0 and offsets[s + 1] = offsets[s] + 5 + grids[s] * grids[s].
All inputs are finite; a program needn't handle non-finite values.
Results may differ from the reference program's by a relative error of at most 0.015.
Values may be sent and summed in bfloat16 or wider, within the bound.
A program may use at most 128 MiB of HBM per device.

```python
import math
import jax
import jax.numpy as jnp
from jax import lax

D = 4096
H = 16
HD = 128
TOK_DEV = 256
G_MIN = 24
G_MAX = 40
HALO = 48
TOKENS = 4096
IMAGES = 2
REACH = 7
N_SEQ = 16
N_TP = 2


def image_layout(key):
    layout_key = jax.random.fold_in(key, 11)
    pair_count = IMAGES // 2
    half_first = jax.random.randint(jax.random.fold_in(layout_key, 1), (pair_count,), G_MIN // 2, G_MAX // 2 + 1)
    chosen = jax.random.randint(jax.random.fold_in(layout_key, 2), (), 0, pair_count)
    half_first = jnp.where(jnp.arange(pair_count) == chosen, G_MAX // 2, half_first)
    first_side = (2 * half_first).astype(jnp.int32)
    room = G_MIN * G_MIN + G_MAX * G_MAX - first_side * first_side
    candidates = (G_MIN + 2 * jnp.arange(1, (G_MAX - G_MIN) // 2 + 1)).astype(jnp.int32)
    fitting = (candidates[None, :] * candidates[None, :] <= room[:, None]).astype(jnp.int32)
    second_side = (G_MIN + 2 * jnp.sum(fitting, axis=1)).astype(jnp.int32)
    flipped = jax.random.randint(jax.random.fold_in(layout_key, 3), (pair_count,), 0, 2)
    side_a = jnp.where(flipped == 1, second_side, first_side)
    side_b = jnp.where(flipped == 1, first_side, second_side)
    sides = jnp.stack([side_a, side_b], axis=1).reshape(IMAGES).astype(jnp.int32)
    lengths = 5 + sides * sides
    starts = jnp.concatenate([jnp.zeros((1,), jnp.int32), jnp.cumsum(lengths).astype(jnp.int32)])
    return (sides, starts)


def draw_grids(key, part):
    return image_layout(key)[0]


def draw_offsets(key, part):
    return image_layout(key)[1]


def draw_w_qkv(key, part):
    normal_draw = jax.random.truncated_normal(key, -4.0, 4.0, (D, H, 3, HD), jnp.float32)
    query_part = normal_draw[:, :, 0] * (1.5 / D ** 0.5)
    key_part = normal_draw[:, :, 1] * (1.5 / D ** 0.5)
    value_part = normal_draw[:, :, 2] * (1.0 / D ** 0.5)
    stacked = jnp.stack([query_part, key_part, value_part], axis=2)
    return jnp.clip(stacked, -3.0, 3.0).astype(jnp.bfloat16)


def level_of(stream_key, extent, cuts, smallest, top_value):
    factor_of, own = 1.0, jax.random.fold_in(stream_key, 6)
    for axis_at, blocks in cuts:
        draws = jnp.exp(jax.random.uniform(jax.random.fold_in(own, axis_at), (blocks,), jnp.float32, smallest / len(cuts), top_value / len(cuts)))
        factor_of = factor_of * jnp.repeat(draws, extent[axis_at] // blocks).reshape([-1 if axis == axis_at else 1 for axis in range(len(extent))])
    return factor_of


def centred(key, shape, deviation, most, split=(), held_as=jnp.bfloat16):
    values = jax.random.normal(key, shape, jnp.float32) * deviation
    if len(split) > 0:
        values = level_of(key, shape, split, -0.22, 0.18) * values
    return jnp.clip(values, min=-most, max=most).astype(held_as)


def setup_inputs(seed: int = 0) -> dict:
    key_list = jax.random.split(jax.random.key(seed), 9)
    tokens = centred(key_list[0], (TOKENS, D), 1.0, 6.0, ((0, 16), (1, 2)))
    ln_gain = jnp.clip(1.0 + 0.18 * jax.random.normal(key_list[1], (D,), jnp.float32), 0.1, 1.9)
    ln_bias = centred(key_list[2], (D,), 0.3, 3.0, (), jnp.float32)
    w_qkv = draw_w_qkv(jax.random.fold_in(key_list[8], 71), 0)
    w_out = centred(key_list[4], (H, HD, D), (H * HD // 4) ** -0.5, 0.25, ((0, 2), (2, 16)))
    layer_scale = jnp.clip(jnp.exp(math.log(2.0) - 1.3862944 * jax.random.uniform(key_list[5], (D,), jnp.float32) ** level_of(key_list[5], (D,), ((0, 2),), -0.2, 0.2)), 0.5, 2.0)
    grids = draw_grids(jax.random.fold_in(key_list[8], 71), 0)
    offsets = draw_offsets(jax.random.fold_in(key_list[8], 71), 0)
    return {"tokens": tokens, "ln_gain": ln_gain, "ln_bias": ln_bias, "w_qkv": w_qkv, "w_out": w_out, "layer_scale": layer_scale, "grids": grids, "offsets": offsets}


def layout_rows(row_ids, offsets, grids, row_count):
    images = grids.shape[0]
    image_ends = offsets[1:]
    segment = lax.optimization_barrier(jnp.sum((row_ids[:, None] >= image_ends[None, :]).astype(jnp.int32), axis=1))
    inside = (row_ids >= 0) & (row_ids < row_count) & (segment < images)
    onehot = (jnp.minimum(segment, images - 1)[:, None] == jnp.arange(images, dtype=jnp.int32)[None, :]).astype(jnp.int32)
    image_start = lax.optimization_barrier(jnp.sum(onehot * offsets[None, :-1], axis=1))
    grid_side = lax.optimization_barrier(jnp.sum(onehot * grids[None, :], axis=1))
    position = row_ids - image_start
    is_patch = inside & (position >= 5)
    patch_index = jnp.maximum(position - 5, 0)
    return (segment, inside, is_patch, patch_index // grid_side, patch_index % grid_side, grid_side)

def rotate(vectors, is_patch, grid_row, grid_col, grid_side):
    quarter = vectors.shape[-1] // 4
    frequency = 2.0 * math.pi * jnp.power(100.0, -jnp.arange(quarter, dtype=jnp.float32) / quarter)
    side_float = grid_side.astype(jnp.float32)
    coord_row = (2 * grid_row + 1).astype(jnp.float32) / side_float - 1.0
    coord_col = (2 * grid_col + 1).astype(jnp.float32) / side_float - 1.0
    angles_row = jnp.where(is_patch[:, None], coord_row[:, None] * frequency[None, :], 0.0)
    angles_col = jnp.where(is_patch[:, None], coord_col[:, None] * frequency[None, :], 0.0)

    def rotate_half(block_vals, angles):
        first_half = block_vals[..., :quarter]
        second_half = block_vals[..., quarter:]
        cosine = jnp.cos(angles)[:, None, :]
        sine_part = jnp.sin(angles)[:, None, :]
        return jnp.concatenate([first_half * cosine - second_half * sine_part, second_half * cosine + first_half * sine_part], axis=-1)
    return jnp.concatenate([rotate_half(vectors[..., :2 * quarter], angles_row), rotate_half(vectors[..., 2 * quarter:], angles_col)], axis=-1)

def attend(query_matrix, block_of_keys, block_of_values, query_segment, query_inside, key_segment, key_inside):
    logit_scale_factor = 1.0 / math.sqrt(query_matrix.shape[-1])
    attention_logits = jnp.einsum('ecn,dcn->ced', query_matrix.astype(jnp.float32), block_of_keys.astype(jnp.float32)) * logit_scale_factor
    allowed = query_inside[:, None] & key_inside[None, :] & (query_segment[:, None] == key_segment[None, :])
    masked = jnp.where(allowed[None], attention_logits, -1e+30)
    row_max = lax.optimization_barrier(jnp.max(masked, axis=2, keepdims=True))
    exp_terms = jnp.where(allowed[None], jnp.exp(masked - row_max), 0.0)
    row_total = lax.optimization_barrier(jnp.sum(exp_terms, axis=2, keepdims=True))
    row_total = jnp.where(query_inside[None, :, None], row_total, 1.0)
    softmax_probabilities = (exp_terms / row_total).astype(jnp.bfloat16)
    attended_output = jnp.einsum('vgm,mvb->gvb', softmax_probabilities.astype(jnp.float32), block_of_values.astype(jnp.float32))
    attended_output = jnp.where(query_inside[:, None, None], attended_output, 0.0)
    return attended_output.astype(jnp.bfloat16)

def reference(tokens, ln_gain, ln_bias, w_qkv, w_out, layer_scale, grids, offsets):
    widened = tokens.astype(jnp.float32)
    average = lax.optimization_barrier(jnp.mean(widened, axis=-1, keepdims=True))
    spread_sq = lax.optimization_barrier(jnp.mean(jnp.square(widened - average), axis=-1, keepdims=True))
    normed = ((widened - average) * lax.rsqrt(spread_sq + 1e-06) * ln_gain + ln_bias).astype(jnp.bfloat16)
    qkv_sums = jnp.dot(normed, w_qkv.reshape(D, H * 3 * HD), preferred_element_type=jnp.float32).reshape(TOKENS, H, 3, HD)
    row_ids = jnp.arange(TOKENS, dtype=jnp.int32)
    segment, inside, is_patch, grid_row, grid_col, grid_side = layout_rows(row_ids, offsets, grids, TOKENS)
    query_matrix = rotate(qkv_sums[:, :, 0], is_patch, grid_row, grid_col, grid_side).astype(jnp.bfloat16)
    roped_keys = rotate(qkv_sums[:, :, 1], is_patch, grid_row, grid_col, grid_side).astype(jnp.bfloat16)
    values = qkv_sums[:, :, 2].astype(jnp.bfloat16)
    margin = REACH * TOK_DEV
    window = (2 * REACH + 1) * TOK_DEV
    padding = jnp.zeros((margin, H, HD), jnp.bfloat16)
    padded_keys = jnp.concatenate([padding, roped_keys, padding], axis=0)
    padded_values = jnp.concatenate([padding, values, padding], axis=0)

    def one_block(block):
        begin = (block * TOK_DEV).astype(jnp.int32)
        block_queries = lax.dynamic_slice_in_dim(query_matrix, begin, TOK_DEV, 0)
        block_keys = lax.dynamic_slice_in_dim(padded_keys, begin, window, 0)
        block_values = lax.dynamic_slice_in_dim(padded_values, begin, window, 0)
        query_rows = begin + jnp.arange(TOK_DEV, dtype=jnp.int32)
        key_rows = begin - margin + jnp.arange(window, dtype=jnp.int32)
        query_layout = layout_rows(query_rows, offsets, grids, TOKENS)
        key_layout = layout_rows(key_rows, offsets, grids, TOKENS)
        return attend(block_queries, block_keys, block_values, query_layout[0], query_layout[1], key_layout[0], key_layout[1])
    attended_output = lax.map(one_block, jnp.arange(N_SEQ, dtype=jnp.int32)).reshape(TOKENS, H, HD)
    group_heads = H // N_TP
    head_total = jnp.zeros((TOKENS, D), jnp.float32)
    for group in range(N_TP):
        share = jnp.dot(attended_output[:, group * group_heads:(group + 1) * group_heads].reshape(TOKENS, group_heads * HD), w_out[group * group_heads:(group + 1) * group_heads].reshape(group_heads * HD, D), preferred_element_type=jnp.float32)
        share = lax.optimization_barrier(share.astype(jnp.bfloat16)).astype(jnp.float32)
        head_total = head_total + share
    layer_out = (widened + layer_scale * head_total).astype(jnp.bfloat16)
    extended = jnp.concatenate([layer_out, jnp.zeros((HALO, D), jnp.bfloat16)], axis=0)
    is_corner = is_patch & (grid_row % 2 == 0) & (grid_col % 2 == 0)
    corner_index = jnp.stack([row_ids, row_ids + 1, row_ids + grid_side, row_ids + grid_side + 1], axis=1)
    corner_index = jnp.clip(corner_index, 0, TOKENS + HALO - 1).astype(jnp.int32)
    merged = jnp.take(extended, corner_index, axis=0)
    return jnp.where(is_corner[:, None, None], merged, jnp.zeros_like(merged))
```

```python
import math

import jax
import jax.numpy as jnp
from jax import lax
from jax.experimental import pallas as pl
from jax.experimental.pallas import tpu as pltpu
from jax.sharding import PartitionSpec as P

HALO = 48
REACH = 7


def from_behind(shard, axis, by):
    count = lax.axis_size(axis)
    pairs = [(i, i + by) for i in range(count) if 0 <= i + by < count]
    return lax.ppermute(shard, axis, pairs)


def layout_rows(row_ids, offsets, grids, row_count):
    images = grids.shape[0]
    image_ends = offsets[1:]
    segment = jnp.sum((row_ids[:, None] >= image_ends[None, :]).astype(jnp.int32), axis=1)
    inside = (row_ids >= 0) & (row_ids < row_count) & (segment < images)
    onehot = (
        jnp.minimum(segment, images - 1)[:, None] == jnp.arange(images, dtype=jnp.int32)[None, :]
    ).astype(jnp.int32)
    image_start = jnp.sum(onehot * offsets[None, :-1], axis=1)
    grid_side = jnp.sum(onehot * grids[None, :], axis=1)
    position = row_ids - image_start
    is_patch = inside & (position >= 5)
    patch_index = jnp.maximum(position - 5, 0)
    return (segment, inside, is_patch, patch_index // grid_side, patch_index % grid_side, grid_side)


def rotate(vectors, is_patch, grid_row, grid_col, grid_side):
    quarter = vectors.shape[-1] // 4
    frequency = 2.0 * math.pi * jnp.power(100.0, -jnp.arange(quarter, dtype=jnp.float32) / quarter)
    side_float = grid_side.astype(jnp.float32)
    coord_row = (2 * grid_row + 1).astype(jnp.float32) / side_float - 1.0
    coord_col = (2 * grid_col + 1).astype(jnp.float32) / side_float - 1.0
    angles_row = jnp.where(is_patch[:, None], coord_row[:, None] * frequency[None, :], 0.0)
    angles_col = jnp.where(is_patch[:, None], coord_col[:, None] * frequency[None, :], 0.0)

    def rotate_half(block_vals, angles):
        first_half = block_vals[..., :quarter]
        second_half = block_vals[..., quarter:]
        cosine = jnp.cos(angles)[:, None, :]
        sine_part = jnp.sin(angles)[:, None, :]
        return jnp.concatenate(
            [
                first_half * cosine - second_half * sine_part,
                second_half * cosine + first_half * sine_part,
            ],
            axis=-1,
        )

    return jnp.concatenate(
        [
            rotate_half(vectors[..., : 2 * quarter], angles_row),
            rotate_half(vectors[..., 2 * quarter :], angles_col),
        ],
        axis=-1,
    )


def attend_blocks(query_matrix, kv_blocks, key_segment, key_inside, query_segment, query_inside):
    logit_scale_factor = 1.0 / math.sqrt(query_matrix.shape[-1])
    rows_here = query_matrix.shape[0]
    heads_here = query_matrix.shape[1]

    def block_scores(block_of_keys, segment_block, inside_block):
        attention_logits = (
            jnp.einsum(
                "ecn,dcn->ced", query_matrix, block_of_keys, preferred_element_type=jnp.float32
            )
            * logit_scale_factor
        )
        allowed = (
            query_inside[:, None]
            & inside_block[None, :]
            & (query_segment[:, None] == segment_block[None, :])
        )
        return (jnp.where(allowed[None], attention_logits, -1e30), allowed)

    def max_step(carry, input_block_rows):
        row_max, row_total = carry
        masked, allowed = block_scores(
            input_block_rows[0][:, 0], input_block_rows[1], input_block_rows[2]
        )
        new_max = jnp.maximum(row_max, jnp.max(masked, axis=2, keepdims=True))
        exp_terms = jnp.where(allowed[None], jnp.exp(masked - new_max), 0.0)
        row_total = row_total * jnp.exp(row_max - new_max) + jnp.sum(
            exp_terms, axis=2, keepdims=True
        )
        return ((new_max, row_total), None)

    start_max = jnp.full((heads_here, rows_here, 1), -1e30, jnp.float32)
    start_total = jnp.zeros((heads_here, rows_here, 1), jnp.float32)
    (row_max, row_total), _ = lax.scan(
        max_step, (start_max, start_total), (kv_blocks, key_segment, key_inside)
    )
    row_total = jnp.where(query_inside[None, :, None], row_total, 1.0)

    def sum_step(running, input_block_rows):
        masked, allowed = block_scores(
            input_block_rows[0][:, 0], input_block_rows[1], input_block_rows[2]
        )
        exp_terms = jnp.where(allowed[None], jnp.exp(masked - row_max), 0.0)
        softmax_probabilities = (exp_terms / row_total).astype(jnp.bfloat16)
        return (
            running
            + jnp.einsum(
                "vgm,mvb->gvb",
                softmax_probabilities,
                input_block_rows[0][:, 1],
                preferred_element_type=jnp.float32,
            ),
            None,
        )

    start_sum = jnp.zeros((rows_here, heads_here, query_matrix.shape[2]), jnp.float32)
    attended_output, _ = lax.scan(sum_step, start_sum, (kv_blocks, key_segment, key_inside))
    attended_output = jnp.where(query_inside[:, None, None], attended_output, 0.0)
    return attended_output.astype(jnp.bfloat16)


def window_body(tokens, ln_gain, ln_bias, w_qkv, w_out, layer_scale, grids, offsets):
    rows_here = tokens.shape[0]
    row_count = rows_here * lax.axis_size("seq")
    first_row = lax.axis_index("seq") * rows_here
    gathered = lax.all_gather(tokens, "tp", axis=1, tiled=True)
    widened = gathered.astype(jnp.float32)
    average = jnp.mean(widened, axis=-1, keepdims=True)
    spread_sq = jnp.mean(jnp.square(widened - average), axis=-1, keepdims=True)
    normed = ((widened - average) * lax.rsqrt(spread_sq + 1e-06) * ln_gain + ln_bias).astype(
        jnp.bfloat16
    )
    qkv_sums = jnp.einsum(
        "td,dhcf->thcf",
        normed,
        lax.all_gather(w_qkv, "seq", axis=0, tiled=True),
        preferred_element_type=jnp.float32,
    )
    row_ids = first_row + jnp.arange(rows_here, dtype=jnp.int32)
    segment, inside, is_patch, grid_row, grid_col, grid_side = layout_rows(
        row_ids, offsets, grids, row_count
    )
    query_matrix = rotate(qkv_sums[:, :, 0], is_patch, grid_row, grid_col, grid_side).astype(
        jnp.bfloat16
    )
    roped_keys = rotate(qkv_sums[:, :, 1], is_patch, grid_row, grid_col, grid_side).astype(
        jnp.bfloat16
    )
    values = qkv_sums[:, :, 2].astype(jnp.bfloat16)
    key_value = jnp.stack([roped_keys, values], axis=1)
    block_count = 2 * REACH + 1
    pieces = []
    for block_slot in range(block_count):
        distance = REACH - block_slot
        if distance == 0:
            pieces.append(key_value)
        else:
            pieces.append(from_behind(key_value, "seq", distance))
    kv_blocks = jnp.stack(pieces, axis=0)
    key_rows = first_row - REACH * rows_here + jnp.arange(block_count * rows_here, dtype=jnp.int32)
    key_layout = layout_rows(key_rows, offsets, grids, row_count)
    key_segment = key_layout[0].reshape(block_count, rows_here)
    key_inside = key_layout[1].reshape(block_count, rows_here)
    attended_output = attend_blocks(
        query_matrix, kv_blocks, key_segment, key_inside, segment, inside
    )
    projected = jnp.einsum(
        "thf,hfc->tc",
        attended_output,
        lax.all_gather(w_out, "seq", axis=2, tiled=True),
        preferred_element_type=jnp.float32,
    )
    head_share = lax.psum_scatter(
        projected.astype(jnp.bfloat16), "tp", scatter_dimension=1, tiled=True
    ).astype(jnp.float32)
    layer_out = (tokens.astype(jnp.float32) + layer_scale * head_share).astype(jnp.bfloat16)
    next_rows = from_behind(layer_out[:HALO], "seq", -1)
    extended = jnp.concatenate([layer_out, next_rows], axis=0)
    is_corner = is_patch & (grid_row % 2 == 0) & (grid_col % 2 == 0)
    local_ids = jnp.arange(rows_here, dtype=jnp.int32)
    corner_index = jnp.stack(
        [local_ids, local_ids + 1, local_ids + grid_side, local_ids + grid_side + 1], axis=1
    )
    corner_index = jnp.clip(corner_index, 0, extended.shape[0] - 1)
    merged = jnp.take(extended, corner_index, axis=0)
    return jnp.where(is_corner[:, None, None], merged, jnp.zeros_like(merged))


PAIR_ROWS = 24 * 24 + 40 * 40 + 10
MESH = pl.DeviceIdType.MESH


def greet(seq, s, t, across):
    barrier = pltpu.get_barrier_semaphore()

    @pl.loop(1, seq)
    def _(i):
        pl.semaphore_signal(
            barrier, inc=1, device_id=(lax.rem(s + i, seq), t), device_id_type=MESH
        )

    if across:
        pl.semaphore_signal(barrier, inc=1, device_id=(s, 1 - t), device_id_type=MESH)
    pl.semaphore_wait(barrier, seq - 1 + across)


def gather_kernel(
    seq, tail, tok_ref, w_ref, x_ref, wg_ref, own_sem, tsend, trecv, wown, wsend, wrecv, fsend, frecv
):
    s = lax.axis_index("seq")
    t = lax.axis_index("tp")
    z, y, c = s // 4, (s // 2) % 2, s % 2
    y_side = s + 2 - 4 * y
    core_side = s + 1 - 2 * c
    rows, width = tok_ref.shape
    half_width = width // 2
    pairs = seq // 2
    head_width = wg_ref.shape[1]
    depth = w_ref.shape[0]
    pending = []

    def when(cond, act):
        if cond is True:
            act()
        else:
            pl.when(cond)(act)

    def both(*conds):
        out = True
        for cond in conds:
            if cond is not True:
                out = cond if out is True else jnp.logical_and(out, cond)
        return out

    def count(zp):
        return rows if zp < 2 else tail

    def move(zp, yp, xp, half, way, device):
        row = pl.multiple_of(2 * rows * zp + (rows * yp if zp < 2 else 0), 16)
        column = pl.multiple_of(width * xp + half_width * half, 128)
        part = x_ref.at[pl.ds(row, count(zp)), pl.ds(column, half_width)]
        at = ((zp * 2 + yp) * 2 + xp) * 2 + half
        return pltpu.make_async_remote_copy(
            src_ref=part,
            dst_ref=part,
            send_sem=tsend.at[at, way],
            recv_sem=trecv.at[at],
            device_id=device,
            device_id_type=MESH,
        )

    def send(cond, copy):
        when(cond, copy.start)
        pending.append((cond, copy))

    def core_has(zp):
        return True if zp < 2 else c == 0

    def row_has(zp, near):
        if zp < 2:
            return True
        return y == 0 if near else y == 1

    greet(seq, s, t, 1)

    for zp in range(3):
        row = pl.multiple_of(2 * rows * zp + (rows * y if zp < 2 else 0), 16)
        own = pltpu.make_async_copy(
            tok_ref.at[pl.ds(0, count(zp)), :],
            x_ref.at[pl.ds(row, count(zp)), pl.ds(pl.multiple_of(width * t, 128), width)],
            own_sem,
        )
        cond = both(core_has(zp), row_has(zp, True), z == zp)
        when(cond, own.start)
        when(cond, own.wait)

    def spread(zp, half, base):
        send(both(base, z >= zp, z < 3), move(zp, y, t, half, 0, (lax.rem(s + 4, seq), t)))
        send(both(base, z <= zp, z > 0), move(zp, y, t, half, 1, (lax.rem(s + seq - 4, seq), t)))
        first, second = (2, 3) if half == 0 else (3, 2)
        for way in (first, second):
            device = (y_side, t) if way == 2 else (s, 1 - t)
            send(base, move(zp, y, t, half, way, device))

    for zp in range(3):
        for half in range(2):
            spread(zp, half, both(core_has(zp), row_has(zp, True), z == zp))

    def slab(source, head_at, send_sem, recv_sem, device):
        return pltpu.make_async_remote_copy(
            src_ref=w_ref.at[:, pl.ds(pl.multiple_of(head_at * head_width, 128), head_width)],
            dst_ref=wg_ref.at[pl.ds(pl.multiple_of(source * depth, 128), depth), :],
            send_sem=send_sem,
            recv_sem=recv_sem,
            device_id=device,
            device_id_type=MESH,
        )

    me = s // 2
    mine = pltpu.make_async_copy(
        w_ref.at[:, pl.ds(pl.multiple_of(me * head_width, 128), head_width)],
        wg_ref.at[pl.ds(pl.multiple_of(s * depth, 128), depth), :],
        wown,
    )
    mine.start()

    def pair_at(step):
        return lax.rem(me + step, pairs)

    for step in range(1, pairs):
        to = pair_at(step)
        slab(s, to, wsend.at[step], wrecv.at[step], (2 * to + c, t)).start()

    def onward(source, step):
        part = wg_ref.at[pl.ds(pl.multiple_of(source * depth, 128), depth), :]
        return pltpu.make_async_remote_copy(
            src_ref=part,
            dst_ref=part,
            send_sem=fsend.at[step],
            recv_sem=frecv.at[step],
            device_id=(core_side, t),
            device_id_type=MESH,
        )

    for zp in (1, 0, 2):
        for half in range(2):
            base = both(core_has(zp), row_has(zp, True), z != zp)
            when(base, move(zp, y, t, half, 0, (s, 1 - t)).wait_recv)
            spread(zp, half, base)
        near = both(core_has(zp), row_has(zp, True))
        far = both(core_has(zp), row_has(zp, False))
        when(far, move(zp, 1 - y, t, 0, 0, (s, 1 - t)).wait_recv)
        send(far, move(zp, 1 - y, t, 0, 3, (s, 1 - t)))
        when(near, move(zp, y, 1 - t, 1, 0, (s, 1 - t)).wait_recv)
        send(near, move(zp, y, 1 - t, 1, 2, (y_side, t)))

    mine.wait()
    onward(s, 0).start()
    for step in range(1, pairs):
        source = 2 * lax.rem(me + pairs - step, pairs) + c
        slab(source, 0, wsend.at[step], wrecv.at[step], (core_side, t)).wait_recv()
        onward(source, step).start()

    for zp in (1, 0, 2):
        near = both(core_has(zp), row_has(zp, True))
        far = both(core_has(zp), row_has(zp, False))
        when(near, move(zp, y, 1 - t, 0, 0, (s, 1 - t)).wait_recv)
        when(far, move(zp, 1 - y, 1 - t, 0, 0, (s, 1 - t)).wait_recv)
        when(far, move(zp, 1 - y, t, 1, 0, (s, 1 - t)).wait_recv)
        when(far, move(zp, 1 - y, 1 - t, 1, 0, (s, 1 - t)).wait_recv)
    for step in range(pairs):
        source = 2 * lax.rem(me + pairs - step, pairs) + c
        onward(source, step).wait_send()
        onward(source + 1 - 2 * c, step).wait_recv()
        if step:
            to = pair_at(step)
            slab(s, to, wsend.at[step], wrecv.at[step], (2 * to + c, t)).wait_send()
    for cond, copy in pending:
        when(cond, copy.wait_send)


def gather_inputs(tokens, weights, seq, tail):
    rows, width = tokens.shape
    head_width = weights.shape[1] // (seq // 2)
    dma = pltpu.SemaphoreType.DMA
    return pl.pallas_call(
        lambda *refs: gather_kernel(seq, tail, *refs),
        out_shape=(
            jax.ShapeDtypeStruct((4 * rows + tail, 2 * width), tokens.dtype),
            jax.ShapeDtypeStruct((weights.shape[0] * seq, head_width), weights.dtype),
        ),
        in_specs=[pl.BlockSpec(memory_space=pl.ANY)] * 2,
        out_specs=[pl.BlockSpec(memory_space=pl.ANY)] * 2,
        scratch_shapes=[
            dma,
            dma((24, 4)),
            dma((24,)),
            dma,
            dma((seq // 2,)),
            dma((seq // 2,)),
            dma((seq // 2,)),
            dma((seq // 2,)),
        ],
        compiler_params=pltpu.CompilerParams(collective_id=0, has_side_effects=True),
        name="gather_inputs",
    )(tokens, weights)


def owners_kernel(seq, rows, tail, att_ref, out_ref, own_sem, msend, mrecv, hsend, hrecv):
    s = lax.axis_index("seq")
    t = lax.axis_index("tp")
    c = s % 2
    head = s // 2
    pairs = seq // 2
    size = att_ref.shape[1]
    greet(seq, s, t, 0)

    def place(head_at):
        return pl.ds(pl.multiple_of(head_at * size, 128), size)

    def main(slot, number, from_head, device):
        return pltpu.make_async_remote_copy(
            src_ref=att_ref.at[pl.ds(rows * slot, number), :],
            dst_ref=out_ref.at[pl.ds(0, number), place(from_head)],
            send_sem=msend.at[slot],
            recv_sem=mrecv.at[from_head],
            device_id=device,
            device_id_type=MESH,
        )

    def halo(slot, from_head, device):
        return pltpu.make_async_remote_copy(
            src_ref=att_ref.at[pl.ds(rows * slot, HALO), :],
            dst_ref=out_ref.at[pl.ds(rows, HALO), place(from_head)],
            send_sem=hsend.at[slot],
            recv_sem=hrecv.at[from_head],
            device_id=device,
            device_id_type=MESH,
        )

    def each_slot(remote_act, local_act, halo_act):
        for slot in range(5):
            number = rows if slot < 4 else tail
            owner = 2 * slot + c
            there = True if slot < 4 else c == 0
            away = jnp.logical_and(owner != s, there)
            here = jnp.logical_and(owner == s, there)
            copy = main(slot, number, head, (owner, t))
            pl.when(away)(lambda: remote_act(copy))
            own = pltpu.make_async_copy(
                att_ref.at[pl.ds(rows * slot, number), :],
                out_ref.at[pl.ds(0, number), place(head)],
                own_sem,
            )
            pl.when(here)(lambda: local_act(own))
            edge = halo(slot, head, (lax.rem(owner + seq - 1, seq), t))
            pl.when(jnp.logical_and(owner >= 1, there))(lambda: halo_act(edge))

    each_slot(lambda copy: copy.start(), lambda own: own.start(), lambda edge: edge.start())

    for from_head in range(pairs):
        sender = 2 * from_head + c
        for number, cond in ((rows, s < 8), (tail, s == 8)):
            arrived = main(0, number, from_head, (lax.rem(s + 1, seq), t))
            pl.when(jnp.logical_and(cond, sender != s))(arrived.wait_recv)
        pl.when(s < 8)(halo(0, from_head, (lax.rem(s + 1, seq), t)).wait_recv)

    each_slot(lambda copy: copy.wait_send(), lambda own: own.wait(), lambda edge: edge.wait_send())


def to_owners(attended, seq, rows, tail):
    dma = pltpu.SemaphoreType.DMA
    pairs = seq // 2
    return pl.pallas_call(
        lambda *refs: owners_kernel(seq, rows, tail, *refs),
        out_shape=jax.ShapeDtypeStruct((rows + HALO, pairs * attended.shape[1]), attended.dtype),
        in_specs=[pl.BlockSpec(memory_space=pl.ANY)],
        out_specs=pl.BlockSpec(memory_space=pl.ANY),
        scratch_shapes=[dma, dma((5,)), dma((pairs,)), dma((5,)), dma((pairs,))],
        compiler_params=pltpu.CompilerParams(collective_id=1, has_side_effects=True),
        name="to_owners",
    )(attended)


def head_body(tokens, ln_gain, ln_bias, w_qkv, w_out, layer_scale, grids, offsets):
    rows, width = tokens.shape
    seq = lax.axis_size("seq")
    row_count = rows * seq
    s = lax.axis_index("seq")
    tp = lax.axis_index("tp")
    core = s % 2
    tail = -(-(PAIR_ROWS - 8 * rows) // 16) * 16
    token_halo = from_behind(tokens[:HALO], "seq", -1)
    out_weights = lax.all_gather(w_out, "seq", axis=2, tiled=True)
    gathered, weights = gather_inputs(tokens, w_qkv.reshape(w_qkv.shape[0], -1), seq, tail)
    widened = gathered.astype(jnp.float32)
    average = jnp.mean(widened, axis=-1, keepdims=True)
    spread_sq = jnp.mean(jnp.square(widened - average), axis=-1, keepdims=True)
    normed = ((widened - average) * lax.rsqrt(spread_sq + 1e-06) * ln_gain + ln_bias).astype(
        jnp.bfloat16
    )
    size = weights.shape[1] // 3
    qkv_sums = jnp.dot(normed, weights, preferred_element_type=jnp.float32).reshape(-1, 3, size)

    slot_rows = jnp.arange(gathered.shape[0], dtype=jnp.int32)
    base_rows = (slot_rows // rows) * (2 * rows) + slot_rows % rows
    row_ids = base_rows + core * rows
    other_ids = base_rows + (1 - core) * rows
    segment, inside, is_patch, grid_row, grid_col, grid_side = layout_rows(
        row_ids, offsets, grids, row_count
    )
    turned = rotate(qkv_sums[:, :2], is_patch, grid_row, grid_col, grid_side)
    queries = turned[:, 0].astype(jnp.bfloat16)
    keys_values = jnp.concatenate([turned[:, 1], qkv_sums[:, 2]], axis=-1).astype(jnp.bfloat16)
    keys_values = jnp.where(inside[:, None], keys_values, jnp.zeros_like(keys_values))
    others = lax.ppermute(keys_values, "seq", [(i, i ^ 1) for i in range(seq)])
    all_kv = jnp.concatenate([keys_values, others], axis=0)
    other_layout = layout_rows(other_ids, offsets, grids, row_count)
    key_segment = jnp.concatenate([segment, other_layout[0]])
    key_inside = jnp.concatenate([inside, other_layout[1]])
    allowed = inside[:, None] & key_inside[None, :] & (segment[:, None] == key_segment[None, :])
    logits = jnp.dot(
        queries, all_kv[:, :size].T, preferred_element_type=jnp.float32
    ) * (1.0 / math.sqrt(size))
    masked = jnp.where(allowed, logits, -1e30)
    row_max = jnp.max(masked, axis=1, keepdims=True)
    terms = jnp.where(allowed, jnp.exp(masked - row_max), 0.0)
    total = jnp.where(inside[:, None], jnp.sum(terms, axis=1, keepdims=True), 1.0)
    soft = (terms / total).astype(jnp.bfloat16)
    attended = jnp.dot(soft, all_kv[:, size:], preferred_element_type=jnp.float32)
    attended = jnp.where(inside[:, None], attended, 0.0).astype(jnp.bfloat16)

    mine = to_owners(attended, seq, rows, tail)
    projected = jnp.dot(
        mine, out_weights.reshape(mine.shape[1], -1), preferred_element_type=jnp.float32
    ).astype(jnp.bfloat16)
    kept = lax.dynamic_slice_in_dim(projected, tp * width, width, 1)
    given = lax.dynamic_slice_in_dim(projected, (1 - tp) * width, width, 1)
    taken = lax.ppermute(given, "tp", [(0, 1), (1, 0)])
    head_total = kept.astype(jnp.float32) + taken.astype(jnp.float32)
    extended_tokens = jnp.concatenate([tokens, token_halo], axis=0).astype(jnp.float32)
    extended = (extended_tokens + layer_scale * head_total).astype(jnp.bfloat16)

    local_ids = jnp.arange(rows, dtype=jnp.int32)
    _, _, is_patch, grid_row, grid_col, grid_side = layout_rows(
        s * rows + local_ids, offsets, grids, row_count
    )
    is_corner = is_patch & (grid_row % 2 == 0) & (grid_col % 2 == 0)
    corner_index = jnp.stack(
        [local_ids, local_ids + 1, local_ids + grid_side, local_ids + grid_side + 1], axis=1
    )
    corner_index = jnp.clip(corner_index, 0, extended.shape[0] - 1)
    merged = jnp.take(extended, corner_index, axis=0)
    return jnp.where(is_corner[:, None, None], merged, jnp.zeros_like(merged))


def solution(mesh):
    placed = (
        P("seq", "tp"),
        P(),
        P(),
        P("seq", "tp", None, None),
        P("tp", None, "seq"),
        P("tp"),
        P(),
        P(),
    )
    small = mesh.shape["seq"] == 16 and mesh.shape["tp"] == 2
    return jax.shard_map(
        head_body if small else window_body,
        mesh=mesh,
        in_specs=placed,
        out_specs=P("seq", None, "tp"),
        check_vma=False,
    )
```

```python
import math

import jax
import jax.numpy as jnp
from jax import lax
from jax.experimental import pallas as pl
from jax.experimental.pallas import tpu as pltpu
from jax.sharding import PartitionSpec as P

HALO = 48
REACH = 7


def from_behind(shard, axis, by):
    count = lax.axis_size(axis)
    pairs = [(i, i + by) for i in range(count) if 0 <= i + by < count]
    return lax.ppermute(shard, axis, pairs)


def layout_rows(row_ids, offsets, grids, row_count):
    images = grids.shape[0]
    image_ends = offsets[1:]
    segment = jnp.sum((row_ids[:, None] >= image_ends[None, :]).astype(jnp.int32), axis=1)
    inside = (row_ids >= 0) & (row_ids < row_count) & (segment < images)
    onehot = (
        jnp.minimum(segment, images - 1)[:, None] == jnp.arange(images, dtype=jnp.int32)[None, :]
    ).astype(jnp.int32)
    image_start = jnp.sum(onehot * offsets[None, :-1], axis=1)
    grid_side = jnp.sum(onehot * grids[None, :], axis=1)
    position = row_ids - image_start
    is_patch = inside & (position >= 5)
    patch_index = jnp.maximum(position - 5, 0)
    return (segment, inside, is_patch, patch_index // grid_side, patch_index % grid_side, grid_side)


def rotate(vectors, is_patch, grid_row, grid_col, grid_side):
    quarter = vectors.shape[-1] // 4
    frequency = 2.0 * math.pi * jnp.power(100.0, -jnp.arange(quarter, dtype=jnp.float32) / quarter)
    side_float = grid_side.astype(jnp.float32)
    coord_row = (2 * grid_row + 1).astype(jnp.float32) / side_float - 1.0
    coord_col = (2 * grid_col + 1).astype(jnp.float32) / side_float - 1.0
    angles_row = jnp.where(is_patch[:, None], coord_row[:, None] * frequency[None, :], 0.0)
    angles_col = jnp.where(is_patch[:, None], coord_col[:, None] * frequency[None, :], 0.0)

    def rotate_half(block_vals, angles):
        first_half = block_vals[..., :quarter]
        second_half = block_vals[..., quarter:]
        cosine = jnp.cos(angles)[:, None, :]
        sine_part = jnp.sin(angles)[:, None, :]
        return jnp.concatenate(
            [
                first_half * cosine - second_half * sine_part,
                second_half * cosine + first_half * sine_part,
            ],
            axis=-1,
        )

    return jnp.concatenate(
        [
            rotate_half(vectors[..., : 2 * quarter], angles_row),
            rotate_half(vectors[..., 2 * quarter :], angles_col),
        ],
        axis=-1,
    )


def attend_blocks(query_matrix, kv_blocks, key_segment, key_inside, query_segment, query_inside):
    logit_scale_factor = 1.0 / math.sqrt(query_matrix.shape[-1])
    rows_here = query_matrix.shape[0]
    heads_here = query_matrix.shape[1]

    def block_scores(block_of_keys, segment_block, inside_block):
        attention_logits = (
            jnp.einsum(
                "ecn,dcn->ced", query_matrix, block_of_keys, preferred_element_type=jnp.float32
            )
            * logit_scale_factor
        )
        allowed = (
            query_inside[:, None]
            & inside_block[None, :]
            & (query_segment[:, None] == segment_block[None, :])
        )
        return (jnp.where(allowed[None], attention_logits, -1e30), allowed)

    def max_step(carry, input_block_rows):
        row_max, row_total = carry
        masked, allowed = block_scores(
            input_block_rows[0][:, 0], input_block_rows[1], input_block_rows[2]
        )
        new_max = jnp.maximum(row_max, jnp.max(masked, axis=2, keepdims=True))
        exp_terms = jnp.where(allowed[None], jnp.exp(masked - new_max), 0.0)
        row_total = row_total * jnp.exp(row_max - new_max) + jnp.sum(
            exp_terms, axis=2, keepdims=True
        )
        return ((new_max, row_total), None)

    start_max = jnp.full((heads_here, rows_here, 1), -1e30, jnp.float32)
    start_total = jnp.zeros((heads_here, rows_here, 1), jnp.float32)
    (row_max, row_total), _ = lax.scan(
        max_step, (start_max, start_total), (kv_blocks, key_segment, key_inside)
    )
    row_total = jnp.where(query_inside[None, :, None], row_total, 1.0)

    def sum_step(running, input_block_rows):
        masked, allowed = block_scores(
            input_block_rows[0][:, 0], input_block_rows[1], input_block_rows[2]
        )
        exp_terms = jnp.where(allowed[None], jnp.exp(masked - row_max), 0.0)
        softmax_probabilities = (exp_terms / row_total).astype(jnp.bfloat16)
        return (
            running
            + jnp.einsum(
                "vgm,mvb->gvb",
                softmax_probabilities,
                input_block_rows[0][:, 1],
                preferred_element_type=jnp.float32,
            ),
            None,
        )

    start_sum = jnp.zeros((rows_here, heads_here, query_matrix.shape[2]), jnp.float32)
    attended_output, _ = lax.scan(sum_step, start_sum, (kv_blocks, key_segment, key_inside))
    attended_output = jnp.where(query_inside[:, None, None], attended_output, 0.0)
    return attended_output.astype(jnp.bfloat16)


def window_body(tokens, ln_gain, ln_bias, w_qkv, w_out, layer_scale, grids, offsets):
    rows_here = tokens.shape[0]
    row_count = rows_here * lax.axis_size("seq")
    first_row = lax.axis_index("seq") * rows_here
    gathered = lax.all_gather(tokens, "tp", axis=1, tiled=True)
    widened = gathered.astype(jnp.float32)
    average = jnp.mean(widened, axis=-1, keepdims=True)
    spread_sq = jnp.mean(jnp.square(widened - average), axis=-1, keepdims=True)
    normed = ((widened - average) * lax.rsqrt(spread_sq + 1e-06) * ln_gain + ln_bias).astype(
        jnp.bfloat16
    )
    qkv_sums = jnp.einsum(
        "td,dhcf->thcf",
        normed,
        lax.all_gather(w_qkv, "seq", axis=0, tiled=True),
        preferred_element_type=jnp.float32,
    )
    row_ids = first_row + jnp.arange(rows_here, dtype=jnp.int32)
    segment, inside, is_patch, grid_row, grid_col, grid_side = layout_rows(
        row_ids, offsets, grids, row_count
    )
    query_matrix = rotate(qkv_sums[:, :, 0], is_patch, grid_row, grid_col, grid_side).astype(
        jnp.bfloat16
    )
    roped_keys = rotate(qkv_sums[:, :, 1], is_patch, grid_row, grid_col, grid_side).astype(
        jnp.bfloat16
    )
    values = qkv_sums[:, :, 2].astype(jnp.bfloat16)
    key_value = jnp.stack([roped_keys, values], axis=1)
    block_count = 2 * REACH + 1
    pieces = []
    for block_slot in range(block_count):
        distance = REACH - block_slot
        if distance == 0:
            pieces.append(key_value)
        else:
            pieces.append(from_behind(key_value, "seq", distance))
    kv_blocks = jnp.stack(pieces, axis=0)
    key_rows = first_row - REACH * rows_here + jnp.arange(block_count * rows_here, dtype=jnp.int32)
    key_layout = layout_rows(key_rows, offsets, grids, row_count)
    key_segment = key_layout[0].reshape(block_count, rows_here)
    key_inside = key_layout[1].reshape(block_count, rows_here)
    attended_output = attend_blocks(
        query_matrix, kv_blocks, key_segment, key_inside, segment, inside
    )
    projected = jnp.einsum(
        "thf,hfc->tc",
        attended_output,
        lax.all_gather(w_out, "seq", axis=2, tiled=True),
        preferred_element_type=jnp.float32,
    )
    head_share = lax.psum_scatter(
        projected.astype(jnp.bfloat16), "tp", scatter_dimension=1, tiled=True
    ).astype(jnp.float32)
    layer_out = (tokens.astype(jnp.float32) + layer_scale * head_share).astype(jnp.bfloat16)
    next_rows = from_behind(layer_out[:HALO], "seq", -1)
    extended = jnp.concatenate([layer_out, next_rows], axis=0)
    is_corner = is_patch & (grid_row % 2 == 0) & (grid_col % 2 == 0)
    local_ids = jnp.arange(rows_here, dtype=jnp.int32)
    corner_index = jnp.stack(
        [local_ids, local_ids + 1, local_ids + grid_side, local_ids + grid_side + 1], axis=1
    )
    corner_index = jnp.clip(corner_index, 0, extended.shape[0] - 1)
    merged = jnp.take(extended, corner_index, axis=0)
    return jnp.where(is_corner[:, None, None], merged, jnp.zeros_like(merged))


PAIR_ROWS = 24 * 24 + 40 * 40 + 10
MESH = pl.DeviceIdType.MESH


def greet(seq, s, t):
    barrier = pltpu.get_barrier_semaphore()
    own = 2 * s + t

    @pl.loop(1, 2 * seq)
    def _(i):
        other = lax.rem(own + i, 2 * seq)
        pl.semaphore_signal(
            barrier, inc=1, device_id=(other // 2, lax.rem(other, 2)), device_id_type=MESH
        )

    pl.semaphore_wait(barrier, 2 * seq - 1)


def gather_kernel(
    seq,
    tail,
    tok_ref,
    w_ref,
    o_ref,
    x_ref,
    wg_ref,
    og_ref,
    own_sem,
    tsend,
    trecv,
    wown,
    wsend,
    wrecv,
    fsend,
    frecv,
    osend,
    orecv,
):
    s = lax.axis_index("seq")
    t = lax.axis_index("tp")
    z, y, c = s // 4, (s // 2) % 2, s % 2
    y_side = s + 2 - 4 * y
    core_side = s + 1 - 2 * c
    rows, width = tok_ref.shape
    half_width = width // 2
    pairs = seq // 2
    head_width = wg_ref.shape[1]
    depth = w_ref.shape[0]
    pending = []

    def when(cond, act):
        if cond is True:
            act()
        else:
            pl.when(cond)(act)

    def both(*conds):
        out = True
        for cond in conds:
            if cond is not True:
                out = cond if out is True else jnp.logical_and(out, cond)
        return out

    def count(zp):
        return rows if zp < 2 else tail

    def move(zp, yp, xp, half, way, device):
        row = pl.multiple_of(2 * rows * zp + (rows * yp if zp < 2 else 0), 16)
        column = pl.multiple_of(width * xp + half_width * half, 128)
        part = x_ref.at[pl.ds(row, count(zp)), pl.ds(column, half_width)]
        at = ((zp * 2 + yp) * 2 + xp) * 2 + half
        return pltpu.make_async_remote_copy(
            src_ref=part,
            dst_ref=part,
            send_sem=tsend.at[at, way],
            recv_sem=trecv.at[at],
            device_id=device,
            device_id_type=MESH,
        )

    def send(cond, copy):
        when(cond, copy.start)
        pending.append((cond, copy))

    def core_has(zp):
        return True if zp < 2 else c == 0

    def row_has(zp, near):
        if zp < 2:
            return True
        return y == 0 if near else y == 1

    greet(seq, s, t)

    for zp in range(3):
        row = pl.multiple_of(2 * rows * zp + (rows * y if zp < 2 else 0), 16)
        own = pltpu.make_async_copy(
            tok_ref.at[pl.ds(0, count(zp)), :],
            x_ref.at[pl.ds(row, count(zp)), pl.ds(pl.multiple_of(width * t, 128), width)],
            own_sem,
        )
        cond = both(core_has(zp), row_has(zp, True), z == zp)
        when(cond, own.start)
        when(cond, own.wait)

    def spread(zp, half, base):
        send(both(base, z >= zp, z < 3), move(zp, y, t, half, 0, (lax.rem(s + 4, seq), t)))
        send(both(base, z <= zp, z > 0), move(zp, y, t, half, 1, (lax.rem(s + seq - 4, seq), t)))
        first, second = (2, 3) if half == 0 else (3, 2)
        for way in (first, second):
            device = (y_side, t) if way == 2 else (s, 1 - t)
            send(base, move(zp, y, t, half, way, device))

    for zp in range(3):
        for half in range(2):
            spread(zp, half, both(core_has(zp), row_has(zp, True), z == zp))

    def slab(source, head_at, send_sem, recv_sem, device):
        return pltpu.make_async_remote_copy(
            src_ref=w_ref.at[:, pl.ds(pl.multiple_of(head_at * head_width, 128), head_width)],
            dst_ref=wg_ref.at[pl.ds(pl.multiple_of(source * depth, 128), depth), :],
            send_sem=send_sem,
            recv_sem=recv_sem,
            device_id=device,
            device_id_type=MESH,
        )

    me = s // 2
    mine = pltpu.make_async_copy(
        w_ref.at[:, pl.ds(pl.multiple_of(me * head_width, 128), head_width)],
        wg_ref.at[pl.ds(pl.multiple_of(s * depth, 128), depth), :],
        wown,
    )
    mine.start()

    def pair_at(step):
        return lax.rem(me + step, pairs)

    def send_slabs(upward):
        for step in range(1, pairs):
            to = pair_at(step)
            slab_copy = slab(s, to, wsend.at[step], wrecv.at[step], (2 * to + c, t))
            pl.when((to // 2 > z) if upward else (to // 2 <= z))(slab_copy.start)

    send_slabs(False)

    out_rows, out_columns = o_ref.shape
    piece = out_columns // 2
    goes = [(2 * lax.rem(s, pairs) + u, s // pairs) for u in range(2)]
    comes = pairs * t + s // 2

    def column_block(u, into, device):
        return pltpu.make_async_remote_copy(
            src_ref=o_ref.at[:, pl.ds(piece * u, piece)],
            dst_ref=og_ref.at[pl.ds(pl.multiple_of(out_rows * into, 128), out_rows), :],
            send_sem=osend.at[u],
            recv_sem=orecv.at[into],
            device_id=device,
            device_id_type=MESH,
        )

    def column_blocks(remote_act, local_act):
        for u in range(2):
            to_s, to_t = goes[u]
            stays = jnp.logical_and(to_s == s, to_t == t)
            copy = column_block(u, t, (to_s, to_t))
            local = pltpu.make_async_copy(
                o_ref.at[:, pl.ds(piece * u, piece)],
                og_ref.at[pl.ds(pl.multiple_of(out_rows * t, 128), out_rows), :],
                osend.at[u],
            )
            pl.when(jnp.logical_not(stays))(lambda: remote_act(copy))
            pl.when(stays)(lambda: local_act(local))

    def onward(source, step):
        part = wg_ref.at[pl.ds(pl.multiple_of(source * depth, 128), depth), :]
        return pltpu.make_async_remote_copy(
            src_ref=part,
            dst_ref=part,
            send_sem=fsend.at[step],
            recv_sem=frecv.at[step],
            device_id=(core_side, t),
            device_id_type=MESH,
        )

    for zp in (1, 0, 2):
        for half in range(2):
            base = both(core_has(zp), row_has(zp, True), z != zp)
            when(base, move(zp, y, t, half, 0, (s, 1 - t)).wait_recv)
            spread(zp, half, base)
        near = both(core_has(zp), row_has(zp, True))
        far = both(core_has(zp), row_has(zp, False))
        when(far, move(zp, 1 - y, t, 0, 0, (s, 1 - t)).wait_recv)
        send(far, move(zp, 1 - y, t, 0, 3, (s, 1 - t)))
        when(near, move(zp, y, 1 - t, 1, 0, (s, 1 - t)).wait_recv)
        send(near, move(zp, y, 1 - t, 1, 2, (y_side, t)))

    send_slabs(True)
    column_blocks(lambda copy: copy.start(), lambda local: local.start())
    mine.wait()
    onward(s, 0).start()
    for step in range(1, pairs):
        source = 2 * lax.rem(me + pairs - step, pairs) + c
        slab(source, 0, wsend.at[step], wrecv.at[step], (core_side, t)).wait_recv()
        onward(source, step).start()

    for zp in (1, 0, 2):
        near = both(core_has(zp), row_has(zp, True))
        far = both(core_has(zp), row_has(zp, False))
        when(near, move(zp, y, 1 - t, 0, 0, (s, 1 - t)).wait_recv)
        when(far, move(zp, 1 - y, 1 - t, 0, 0, (s, 1 - t)).wait_recv)
        when(far, move(zp, 1 - y, t, 1, 0, (s, 1 - t)).wait_recv)
        when(far, move(zp, 1 - y, 1 - t, 1, 0, (s, 1 - t)).wait_recv)
    for step in range(pairs):
        source = 2 * lax.rem(me + pairs - step, pairs) + c
        onward(source, step).wait_send()
        onward(source + 1 - 2 * c, step).wait_recv()
        if step:
            to = pair_at(step)
            slab(s, to, wsend.at[step], wrecv.at[step], (2 * to + c, t)).wait_send()
    column_blocks(lambda copy: copy.wait_send(), lambda local: local.wait())
    for into in range(2):
        remote = jnp.logical_or(comes != s, into != t)
        pl.when(remote)(column_block(0, into, (core_side, t)).wait_recv)
    for cond, copy in pending:
        when(cond, copy.wait_send)


def gather_inputs(tokens, weights, out_weights, seq, tail):
    rows, width = tokens.shape
    head_width = weights.shape[1] // (seq // 2)
    dma = pltpu.SemaphoreType.DMA
    return pl.pallas_call(
        lambda *refs: gather_kernel(seq, tail, *refs),
        out_shape=(
            jax.ShapeDtypeStruct((4 * rows + tail, 2 * width), tokens.dtype),
            jax.ShapeDtypeStruct((weights.shape[0] * seq, head_width), weights.dtype),
            jax.ShapeDtypeStruct(
                (2 * out_weights.shape[0], out_weights.shape[1] // 2), weights.dtype
            ),
        ),
        in_specs=[pl.BlockSpec(memory_space=pl.ANY)] * 3,
        out_specs=[pl.BlockSpec(memory_space=pl.ANY)] * 3,
        scratch_shapes=[
            dma,
            dma((24, 4)),
            dma((24,)),
            dma,
            dma((seq // 2,)),
            dma((seq // 2,)),
            dma((seq // 2,)),
            dma((seq // 2,)),
            dma((2,)),
            dma((2,)),
        ],
        compiler_params=pltpu.CompilerParams(collective_id=0, has_side_effects=True),
        name="gather_inputs",
    )(tokens, weights, out_weights)


def owners_kernel(seq, rows, tail, att_ref, out_ref, own_sem, msend, mrecv, hsend, hrecv):
    s = lax.axis_index("seq")
    t = lax.axis_index("tp")
    c = s % 2
    pairs = seq // 2
    head = pairs * t + s // 2
    size = att_ref.shape[1]
    greet(seq, s, t)

    def place(head_at):
        return pl.ds(pl.multiple_of(head_at * size, 128), size)

    def main(slot, number, side, from_head, device):
        return pltpu.make_async_remote_copy(
            src_ref=att_ref.at[pl.ds(rows * slot, number), :],
            dst_ref=out_ref.at[pl.ds(0, number), place(from_head)],
            send_sem=msend.at[slot, side],
            recv_sem=mrecv.at[from_head],
            device_id=device,
            device_id_type=MESH,
        )

    def halo(slot, side, from_head, device):
        return pltpu.make_async_remote_copy(
            src_ref=att_ref.at[pl.ds(rows * slot, HALO), :],
            dst_ref=out_ref.at[pl.ds(rows, HALO), place(from_head)],
            send_sem=hsend.at[slot, side],
            recv_sem=hrecv.at[from_head],
            device_id=device,
            device_id_type=MESH,
        )

    def each_slot(remote_act, local_act, halo_act):
        for slot in range(5):
            number = rows if slot < 4 else tail
            owner = 2 * slot + c
            there = True if slot < 4 else c == 0
            own = pltpu.make_async_copy(
                att_ref.at[pl.ds(rows * slot, number), :],
                out_ref.at[pl.ds(0, number), place(head)],
                own_sem,
            )
            pl.when(jnp.logical_and(owner == s, there))(lambda: local_act(own))
            for side in range(2):
                to_t = t if side == 0 else 1 - t
                copy = main(slot, number, side, head, (owner, to_t))
                away = jnp.logical_and(owner != s, there) if side == 0 else there
                pl.when(away)(lambda: remote_act(copy))
                edge = halo(slot, side, head, (lax.rem(owner + seq - 1, seq), to_t))
                pl.when(jnp.logical_and(owner >= 1, there))(lambda: halo_act(edge))

    each_slot(lambda copy: copy.start(), lambda own: own.start(), lambda edge: edge.start())

    for from_head in range(2 * pairs):
        itself = jnp.logical_and(from_head % pairs == s // 2, from_head // pairs == t)
        for number, cond in ((rows, s < 8), (tail, s == 8)):
            arrived = main(0, number, 0, from_head, (s, 1 - t))
            pl.when(jnp.logical_and(cond, jnp.logical_not(itself)))(arrived.wait_recv)
        pl.when(s < 8)(halo(0, 0, from_head, (s, 1 - t)).wait_recv)

    each_slot(lambda copy: copy.wait_send(), lambda own: own.wait(), lambda edge: edge.wait_send())


def to_owners(attended, seq, rows, tail):
    dma = pltpu.SemaphoreType.DMA
    return pl.pallas_call(
        lambda *refs: owners_kernel(seq, rows, tail, *refs),
        out_shape=jax.ShapeDtypeStruct((rows + HALO, seq * attended.shape[1]), attended.dtype),
        in_specs=[pl.BlockSpec(memory_space=pl.ANY)],
        out_specs=pl.BlockSpec(memory_space=pl.ANY),
        scratch_shapes=[dma, dma((5, 2)), dma((seq,)), dma((5, 2)), dma((seq,))],
        compiler_params=pltpu.CompilerParams(collective_id=1, has_side_effects=True),
        name="to_owners",
    )(attended)


def merge_kernel(pick_ref, rows_ref, out_ref):
    count, four, width = out_ref.shape
    picked = jnp.dot(pick_ref[...], rows_ref[...], preferred_element_type=jnp.float32)
    out_ref[...] = picked.reshape(count, four, width).astype(out_ref.dtype)


def merge_rows(pick, extended, count, step):
    width = extended.shape[1]
    return pl.pallas_call(
        merge_kernel,
        grid=(count // step,),
        out_shape=jax.ShapeDtypeStruct((count, 4, width), extended.dtype),
        in_specs=[
            pl.BlockSpec((4 * step, pick.shape[1]), lambda i: (i, 0)),
            pl.BlockSpec(extended.shape, lambda i: (0, 0)),
        ],
        out_specs=pl.BlockSpec((step, 4, width), lambda i: (i, 0, 0)),
        compiler_params=pltpu.CompilerParams(vmem_limit_bytes=32 * 1024 * 1024),
        name="merge_rows",
    )(pick, extended)


def head_body(tokens, ln_gain, ln_bias, w_qkv, w_out, layer_scale, grids, offsets):
    rows, width = tokens.shape
    seq = lax.axis_size("seq")
    row_count = rows * seq
    s = lax.axis_index("seq")
    tp = lax.axis_index("tp")
    core = s % 2
    tail = -(-(PAIR_ROWS - 8 * rows) // 16) * 16
    token_halo = from_behind(tokens[:HALO], "seq", -1)
    gathered, weights, columns = gather_inputs(
        tokens,
        w_qkv.reshape(w_qkv.shape[0], -1),
        w_out.reshape(-1, w_out.shape[2]),
        seq,
        tail,
    )
    out_weights = lax.all_gather(columns, "seq", axis=1, tiled=True)
    widened = gathered.astype(jnp.float32)
    average = jnp.mean(widened, axis=-1, keepdims=True)
    spread_sq = jnp.mean(jnp.square(widened - average), axis=-1, keepdims=True)
    normed = ((widened - average) * lax.rsqrt(spread_sq + 1e-06) * ln_gain + ln_bias).astype(
        jnp.bfloat16
    )
    size = weights.shape[1] // 3
    qkv_sums = jnp.dot(normed, weights, preferred_element_type=jnp.float32).reshape(-1, 3, size)

    slot_rows = jnp.arange(gathered.shape[0], dtype=jnp.int32)
    base_rows = (slot_rows // rows) * (2 * rows) + slot_rows % rows
    row_ids = base_rows + core * rows
    other_ids = base_rows + (1 - core) * rows
    segment, inside, is_patch, grid_row, grid_col, grid_side = layout_rows(
        row_ids, offsets, grids, row_count
    )
    turned = rotate(qkv_sums[:, :2], is_patch, grid_row, grid_col, grid_side)
    queries = turned[:, 0].astype(jnp.bfloat16)
    keys_values = jnp.concatenate([turned[:, 1], qkv_sums[:, 2]], axis=-1).astype(jnp.bfloat16)
    keys_values = jnp.where(inside[:, None], keys_values, jnp.zeros_like(keys_values))
    others = lax.ppermute(keys_values, "seq", [(i, i ^ 1) for i in range(seq)])
    all_kv = jnp.concatenate([keys_values, others], axis=0)
    other_layout = layout_rows(other_ids, offsets, grids, row_count)
    key_segment = jnp.concatenate([segment, other_layout[0]])
    key_inside = jnp.concatenate([inside, other_layout[1]])
    allowed = inside[:, None] & key_inside[None, :] & (segment[:, None] == key_segment[None, :])
    logits = jnp.dot(
        queries, all_kv[:, :size].T, preferred_element_type=jnp.float32
    ) * (1.0 / math.sqrt(size))
    masked = jnp.where(allowed, logits, -1e30)
    row_max = jnp.max(masked, axis=1, keepdims=True)
    terms = jnp.where(allowed, jnp.exp(masked - row_max), 0.0)
    total = jnp.where(inside[:, None], jnp.sum(terms, axis=1, keepdims=True), 1.0)
    soft = (terms / total).astype(jnp.bfloat16)
    attended = jnp.dot(soft, all_kv[:, size:], preferred_element_type=jnp.float32)
    attended = jnp.where(inside[:, None], attended, 0.0).astype(jnp.bfloat16)

    mine = to_owners(attended, seq, rows, tail)
    head_total = jnp.dot(mine, out_weights, preferred_element_type=jnp.float32)
    extended_tokens = jnp.concatenate([tokens, token_halo], axis=0).astype(jnp.float32)
    extended = (extended_tokens + layer_scale * head_total).astype(jnp.bfloat16)
    extended_ids = s * rows + jnp.arange(rows + HALO, dtype=jnp.int32)
    extended = jnp.where(
        (extended_ids < offsets[-1])[:, None], extended, jnp.zeros_like(extended)
    )

    local_ids = jnp.arange(rows, dtype=jnp.int32)
    _, _, is_patch, grid_row, grid_col, grid_side = layout_rows(
        s * rows + local_ids, offsets, grids, row_count
    )
    is_corner = is_patch & (grid_row % 2 == 0) & (grid_col % 2 == 0)
    corner_index = jnp.stack(
        [local_ids, local_ids + 1, local_ids + grid_side, local_ids + grid_side + 1], axis=1
    )
    corner_index = jnp.where(is_corner[:, None], corner_index, -1).reshape(-1)
    pick = (
        corner_index[:, None] == jnp.arange(extended.shape[0], dtype=jnp.int32)[None, :]
    ).astype(jnp.bfloat16)
    return merge_rows(pick, extended, rows, 32)


def solution(mesh):
    placed = (
        P("seq", "tp"),
        P(),
        P(),
        P("seq", "tp", None, None),
        P("tp", None, "seq"),
        P("tp"),
        P(),
        P(),
    )
    small = mesh.shape["seq"] == 16 and mesh.shape["tp"] == 2
    return jax.shard_map(
        head_body if small else window_body,
        mesh=mesh,
        in_specs=placed,
        out_specs=P("seq", None, "tp"),
        check_vma=False,
    )
```

```python
import math

import jax
import jax.numpy as jnp
from jax import lax
from jax.experimental import pallas as pl
from jax.experimental.pallas import tpu as pltpu
from jax.sharding import PartitionSpec as P

HALO = 48
REACH = 7


def from_behind(shard, axis, by):
    count = lax.axis_size(axis)
    pairs = [(i, i + by) for i in range(count) if 0 <= i + by < count]
    return lax.ppermute(shard, axis, pairs)


def layout_rows(row_ids, offsets, grids, row_count):
    images = grids.shape[0]
    image_ends = offsets[1:]
    segment = jnp.sum((row_ids[:, None] >= image_ends[None, :]).astype(jnp.int32), axis=1)
    inside = (row_ids >= 0) & (row_ids < row_count) & (segment < images)
    onehot = (
        jnp.minimum(segment, images - 1)[:, None] == jnp.arange(images, dtype=jnp.int32)[None, :]
    ).astype(jnp.int32)
    image_start = jnp.sum(onehot * offsets[None, :-1], axis=1)
    grid_side = jnp.sum(onehot * grids[None, :], axis=1)
    position = row_ids - image_start
    is_patch = inside & (position >= 5)
    patch_index = jnp.maximum(position - 5, 0)
    return (segment, inside, is_patch, patch_index // grid_side, patch_index % grid_side, grid_side)


def rotate(vectors, is_patch, grid_row, grid_col, grid_side):
    quarter = vectors.shape[-1] // 4
    frequency = 2.0 * math.pi * jnp.power(100.0, -jnp.arange(quarter, dtype=jnp.float32) / quarter)
    side_float = grid_side.astype(jnp.float32)
    coord_row = (2 * grid_row + 1).astype(jnp.float32) / side_float - 1.0
    coord_col = (2 * grid_col + 1).astype(jnp.float32) / side_float - 1.0
    angles_row = jnp.where(is_patch[:, None], coord_row[:, None] * frequency[None, :], 0.0)
    angles_col = jnp.where(is_patch[:, None], coord_col[:, None] * frequency[None, :], 0.0)

    def rotate_half(block_vals, angles):
        first_half = block_vals[..., :quarter]
        second_half = block_vals[..., quarter:]
        cosine = jnp.cos(angles)[:, None, :]
        sine_part = jnp.sin(angles)[:, None, :]
        return jnp.concatenate(
            [
                first_half * cosine - second_half * sine_part,
                second_half * cosine + first_half * sine_part,
            ],
            axis=-1,
        )

    return jnp.concatenate(
        [
            rotate_half(vectors[..., : 2 * quarter], angles_row),
            rotate_half(vectors[..., 2 * quarter :], angles_col),
        ],
        axis=-1,
    )


def attend_blocks(query_matrix, kv_blocks, key_segment, key_inside, query_segment, query_inside):
    logit_scale_factor = 1.0 / math.sqrt(query_matrix.shape[-1])
    rows_here = query_matrix.shape[0]
    heads_here = query_matrix.shape[1]

    def block_scores(block_of_keys, segment_block, inside_block):
        attention_logits = (
            jnp.einsum(
                "ecn,dcn->ced", query_matrix, block_of_keys, preferred_element_type=jnp.float32
            )
            * logit_scale_factor
        )
        allowed = (
            query_inside[:, None]
            & inside_block[None, :]
            & (query_segment[:, None] == segment_block[None, :])
        )
        return (jnp.where(allowed[None], attention_logits, -1e30), allowed)

    def max_step(carry, input_block_rows):
        row_max, row_total = carry
        masked, allowed = block_scores(
            input_block_rows[0][:, 0], input_block_rows[1], input_block_rows[2]
        )
        new_max = jnp.maximum(row_max, jnp.max(masked, axis=2, keepdims=True))
        exp_terms = jnp.where(allowed[None], jnp.exp(masked - new_max), 0.0)
        row_total = row_total * jnp.exp(row_max - new_max) + jnp.sum(
            exp_terms, axis=2, keepdims=True
        )
        return ((new_max, row_total), None)

    start_max = jnp.full((heads_here, rows_here, 1), -1e30, jnp.float32)
    start_total = jnp.zeros((heads_here, rows_here, 1), jnp.float32)
    (row_max, row_total), _ = lax.scan(
        max_step, (start_max, start_total), (kv_blocks, key_segment, key_inside)
    )
    row_total = jnp.where(query_inside[None, :, None], row_total, 1.0)

    def sum_step(running, input_block_rows):
        masked, allowed = block_scores(
            input_block_rows[0][:, 0], input_block_rows[1], input_block_rows[2]
        )
        exp_terms = jnp.where(allowed[None], jnp.exp(masked - row_max), 0.0)
        softmax_probabilities = (exp_terms / row_total).astype(jnp.bfloat16)
        return (
            running
            + jnp.einsum(
                "vgm,mvb->gvb",
                softmax_probabilities,
                input_block_rows[0][:, 1],
                preferred_element_type=jnp.float32,
            ),
            None,
        )

    start_sum = jnp.zeros((rows_here, heads_here, query_matrix.shape[2]), jnp.float32)
    attended_output, _ = lax.scan(sum_step, start_sum, (kv_blocks, key_segment, key_inside))
    attended_output = jnp.where(query_inside[:, None, None], attended_output, 0.0)
    return attended_output.astype(jnp.bfloat16)


def window_body(tokens, ln_gain, ln_bias, w_qkv, w_out, layer_scale, grids, offsets):
    rows_here = tokens.shape[0]
    row_count = rows_here * lax.axis_size("seq")
    first_row = lax.axis_index("seq") * rows_here
    gathered = lax.all_gather(tokens, "tp", axis=1, tiled=True)
    widened = gathered.astype(jnp.float32)
    average = jnp.mean(widened, axis=-1, keepdims=True)
    spread_sq = jnp.mean(jnp.square(widened - average), axis=-1, keepdims=True)
    normed = ((widened - average) * lax.rsqrt(spread_sq + 1e-06) * ln_gain + ln_bias).astype(
        jnp.bfloat16
    )
    qkv_sums = jnp.einsum(
        "td,dhcf->thcf",
        normed,
        lax.all_gather(w_qkv, "seq", axis=0, tiled=True),
        preferred_element_type=jnp.float32,
    )
    row_ids = first_row + jnp.arange(rows_here, dtype=jnp.int32)
    segment, inside, is_patch, grid_row, grid_col, grid_side = layout_rows(
        row_ids, offsets, grids, row_count
    )
    query_matrix = rotate(qkv_sums[:, :, 0], is_patch, grid_row, grid_col, grid_side).astype(
        jnp.bfloat16
    )
    roped_keys = rotate(qkv_sums[:, :, 1], is_patch, grid_row, grid_col, grid_side).astype(
        jnp.bfloat16
    )
    values = qkv_sums[:, :, 2].astype(jnp.bfloat16)
    key_value = jnp.stack([roped_keys, values], axis=1)
    block_count = 2 * REACH + 1
    pieces = []
    for block_slot in range(block_count):
        distance = REACH - block_slot
        if distance == 0:
            pieces.append(key_value)
        else:
            pieces.append(from_behind(key_value, "seq", distance))
    kv_blocks = jnp.stack(pieces, axis=0)
    key_rows = first_row - REACH * rows_here + jnp.arange(block_count * rows_here, dtype=jnp.int32)
    key_layout = layout_rows(key_rows, offsets, grids, row_count)
    key_segment = key_layout[0].reshape(block_count, rows_here)
    key_inside = key_layout[1].reshape(block_count, rows_here)
    attended_output = attend_blocks(
        query_matrix, kv_blocks, key_segment, key_inside, segment, inside
    )
    projected = jnp.einsum(
        "thf,hfc->tc",
        attended_output,
        lax.all_gather(w_out, "seq", axis=2, tiled=True),
        preferred_element_type=jnp.float32,
    )
    head_share = lax.psum_scatter(
        projected.astype(jnp.bfloat16), "tp", scatter_dimension=1, tiled=True
    ).astype(jnp.float32)
    layer_out = (tokens.astype(jnp.float32) + layer_scale * head_share).astype(jnp.bfloat16)
    next_rows = from_behind(layer_out[:HALO], "seq", -1)
    extended = jnp.concatenate([layer_out, next_rows], axis=0)
    is_corner = is_patch & (grid_row % 2 == 0) & (grid_col % 2 == 0)
    local_ids = jnp.arange(rows_here, dtype=jnp.int32)
    corner_index = jnp.stack(
        [local_ids, local_ids + 1, local_ids + grid_side, local_ids + grid_side + 1], axis=1
    )
    corner_index = jnp.clip(corner_index, 0, extended.shape[0] - 1)
    merged = jnp.take(extended, corner_index, axis=0)
    return jnp.where(is_corner[:, None, None], merged, jnp.zeros_like(merged))


PAIR_ROWS = 24 * 24 + 40 * 40 + 10
MESH = pl.DeviceIdType.MESH


def greet(seq, s, t):
    barrier = pltpu.get_barrier_semaphore()
    own = 2 * s + t

    @pl.loop(1, 2 * seq)
    def _(i):
        other = lax.rem(own + i, 2 * seq)
        pl.semaphore_signal(
            barrier, inc=1, device_id=(other // 2, lax.rem(other, 2)), device_id_type=MESH
        )

    pl.semaphore_wait(barrier, 2 * seq - 1)


def gather_kernel(
    seq,
    tail,
    tok_ref,
    w_ref,
    o_ref,
    x_ref,
    wg_ref,
    og_ref,
    own_sem,
    tsend,
    trecv,
    wown,
    wsend,
    wrecv,
    fsend,
    frecv,
    osend,
    orecv,
):
    s = lax.axis_index("seq")
    t = lax.axis_index("tp")
    z, y, c = s // 4, (s // 2) % 2, s % 2
    y_side = s + 2 - 4 * y
    core_side = s + 1 - 2 * c
    rows, width = tok_ref.shape
    half_width = width // 2
    pairs = seq // 2
    head_width = wg_ref.shape[1]
    depth = w_ref.shape[0]
    pending = []

    def when(cond, act):
        if cond is True:
            act()
        else:
            pl.when(cond)(act)

    def both(*conds):
        out = True
        for cond in conds:
            if cond is not True:
                out = cond if out is True else jnp.logical_and(out, cond)
        return out

    def count(zp):
        return rows if zp < 2 else tail

    def move(zp, yp, xp, half, way, device):
        row = pl.multiple_of(2 * rows * zp + (rows * yp if zp < 2 else 0), 16)
        column = pl.multiple_of(width * xp + half_width * half, 128)
        part = x_ref.at[pl.ds(row, count(zp)), pl.ds(column, half_width)]
        at = ((zp * 2 + yp) * 2 + xp) * 2 + half
        return pltpu.make_async_remote_copy(
            src_ref=part,
            dst_ref=part,
            send_sem=tsend.at[at, way],
            recv_sem=trecv.at[at],
            device_id=device,
            device_id_type=MESH,
        )

    def send(cond, copy):
        when(cond, copy.start)
        pending.append((cond, copy))

    def core_has(zp):
        return True if zp < 2 else c == 0

    def row_has(zp, near):
        if zp < 2:
            return True
        return y == 0 if near else y == 1

    greet(seq, s, t)

    for zp in range(3):
        row = pl.multiple_of(2 * rows * zp + (rows * y if zp < 2 else 0), 16)
        own = pltpu.make_async_copy(
            tok_ref.at[pl.ds(0, count(zp)), :],
            x_ref.at[pl.ds(row, count(zp)), pl.ds(pl.multiple_of(width * t, 128), width)],
            own_sem,
        )
        cond = both(core_has(zp), row_has(zp, True), z == zp)
        when(cond, own.start)
        when(cond, own.wait)

    def spread(zp, half, base):
        send(both(base, z >= zp, z < 3), move(zp, y, t, half, 0, (lax.rem(s + 4, seq), t)))
        send(both(base, z <= zp, z > 0), move(zp, y, t, half, 1, (lax.rem(s + seq - 4, seq), t)))
        first, second = (2, 3) if half == 0 else (3, 2)
        for way in (first, second):
            device = (y_side, t) if way == 2 else (s, 1 - t)
            send(base, move(zp, y, t, half, way, device))

    for zp in range(3):
        for half in range(2):
            spread(zp, half, both(core_has(zp), row_has(zp, True), z == zp))

    def slab(source, head_at, send_sem, recv_sem, device):
        return pltpu.make_async_remote_copy(
            src_ref=w_ref.at[:, pl.ds(pl.multiple_of(head_at * head_width, 128), head_width)],
            dst_ref=wg_ref.at[pl.ds(pl.multiple_of(source * depth, 128), depth), :],
            send_sem=send_sem,
            recv_sem=recv_sem,
            device_id=device,
            device_id_type=MESH,
        )

    me = s // 2
    mine = pltpu.make_async_copy(
        w_ref.at[:, pl.ds(pl.multiple_of(me * head_width, 128), head_width)],
        wg_ref.at[pl.ds(pl.multiple_of(s * depth, 128), depth), :],
        wown,
    )
    mine.start()

    def pair_at(step):
        return lax.rem(me + step, pairs)

    def send_slabs(upward):
        for step in range(1, pairs):
            to = pair_at(step)
            slab_copy = slab(s, to, wsend.at[step], wrecv.at[step], (2 * to + c, t))
            pl.when((to // 2 > z) if upward else (to // 2 <= z))(slab_copy.start)

    send_slabs(False)

    goes_s, goes_t = 2 * lax.rem(s, pairs) + t, s // pairs
    comes_s, comes_t = pairs * t + s // 2, lax.rem(s, 2)
    out_sends = pltpu.make_async_remote_copy(
        src_ref=o_ref,
        dst_ref=og_ref,
        send_sem=osend,
        recv_sem=orecv,
        device_id=(goes_s, goes_t),
        device_id_type=MESH,
    )
    out_stays = pltpu.make_async_copy(o_ref, og_ref, osend)
    stays = jnp.logical_and(goes_s == s, goes_t == t)
    stayed = jnp.logical_and(comes_s == s, comes_t == t)

    def onward(source, step):
        part = wg_ref.at[pl.ds(pl.multiple_of(source * depth, 128), depth), :]
        return pltpu.make_async_remote_copy(
            src_ref=part,
            dst_ref=part,
            send_sem=fsend.at[step],
            recv_sem=frecv.at[step],
            device_id=(core_side, t),
            device_id_type=MESH,
        )

    for zp in (1, 0, 2):
        for half in range(2):
            base = both(core_has(zp), row_has(zp, True), z != zp)
            when(base, move(zp, y, t, half, 0, (s, 1 - t)).wait_recv)
            spread(zp, half, base)
        near = both(core_has(zp), row_has(zp, True))
        far = both(core_has(zp), row_has(zp, False))
        when(far, move(zp, 1 - y, t, 0, 0, (s, 1 - t)).wait_recv)
        send(far, move(zp, 1 - y, t, 0, 3, (s, 1 - t)))
        when(near, move(zp, y, 1 - t, 1, 0, (s, 1 - t)).wait_recv)
        send(near, move(zp, y, 1 - t, 1, 2, (y_side, t)))

    send_slabs(True)
    pl.when(jnp.logical_not(stays))(out_sends.start)
    pl.when(stays)(out_stays.start)
    mine.wait()
    onward(s, 0).start()
    for step in range(1, pairs):
        source = 2 * lax.rem(me + pairs - step, pairs) + c
        slab(source, 0, wsend.at[step], wrecv.at[step], (core_side, t)).wait_recv()
        onward(source, step).start()

    for zp in (1, 0, 2):
        near = both(core_has(zp), row_has(zp, True))
        far = both(core_has(zp), row_has(zp, False))
        when(near, move(zp, y, 1 - t, 0, 0, (s, 1 - t)).wait_recv)
        when(far, move(zp, 1 - y, 1 - t, 0, 0, (s, 1 - t)).wait_recv)
        when(far, move(zp, 1 - y, t, 1, 0, (s, 1 - t)).wait_recv)
        when(far, move(zp, 1 - y, 1 - t, 1, 0, (s, 1 - t)).wait_recv)
    for step in range(pairs):
        source = 2 * lax.rem(me + pairs - step, pairs) + c
        onward(source, step).wait_send()
        onward(source + 1 - 2 * c, step).wait_recv()
        if step:
            to = pair_at(step)
            slab(s, to, wsend.at[step], wrecv.at[step], (2 * to + c, t)).wait_send()
    pl.when(jnp.logical_not(stays))(out_sends.wait_send)
    pl.when(stays)(out_stays.wait)
    pl.when(jnp.logical_not(stayed))(out_sends.wait_recv)
    for cond, copy in pending:
        when(cond, copy.wait_send)


def gather_inputs(tokens, weights, out_weights, seq, tail):
    rows, width = tokens.shape
    head_width = weights.shape[1] // (seq // 2)
    dma = pltpu.SemaphoreType.DMA
    return pl.pallas_call(
        lambda *refs: gather_kernel(seq, tail, *refs),
        out_shape=(
            jax.ShapeDtypeStruct((4 * rows + tail, 2 * width), tokens.dtype),
            jax.ShapeDtypeStruct((weights.shape[0] * seq, head_width), weights.dtype),
            jax.ShapeDtypeStruct(out_weights.shape, out_weights.dtype),
        ),
        in_specs=[pl.BlockSpec(memory_space=pl.ANY)] * 3,
        out_specs=[pl.BlockSpec(memory_space=pl.ANY)] * 3,
        scratch_shapes=[
            dma,
            dma((24, 4)),
            dma((24,)),
            dma,
            dma((seq // 2,)),
            dma((seq // 2,)),
            dma((seq // 2,)),
            dma((seq // 2,)),
            dma,
            dma,
        ],
        compiler_params=pltpu.CompilerParams(collective_id=0, has_side_effects=True),
        name="gather_inputs",
    )(tokens, weights, out_weights)


def owners_kernel(seq, rows, tail, att_ref, out_ref, own_sem, msend, mrecv, hsend, hrecv):
    s = lax.axis_index("seq")
    t = lax.axis_index("tp")
    c = s % 2
    pairs = seq // 2
    head = pairs * t + s // 2
    size = att_ref.shape[1]
    greet(seq, s, t)

    def place(head_at):
        return pl.ds(pl.multiple_of(head_at * size, 128), size)

    def main(slot, number, side, from_head, device):
        return pltpu.make_async_remote_copy(
            src_ref=att_ref.at[pl.ds(rows * slot, number), :],
            dst_ref=out_ref.at[pl.ds(0, number), place(from_head)],
            send_sem=msend.at[slot, side],
            recv_sem=mrecv.at[from_head],
            device_id=device,
            device_id_type=MESH,
        )

    def halo(slot, side, from_head, device):
        return pltpu.make_async_remote_copy(
            src_ref=att_ref.at[pl.ds(rows * slot, HALO), :],
            dst_ref=out_ref.at[pl.ds(rows, HALO), place(from_head)],
            send_sem=hsend.at[slot, side],
            recv_sem=hrecv.at[from_head],
            device_id=device,
            device_id_type=MESH,
        )

    def each_slot(remote_act, local_act, halo_act):
        for slot in range(5):
            number = rows if slot < 4 else tail
            owner = 2 * slot + c
            there = True if slot < 4 else c == 0
            own = pltpu.make_async_copy(
                att_ref.at[pl.ds(rows * slot, number), :],
                out_ref.at[pl.ds(0, number), place(head)],
                own_sem,
            )
            pl.when(jnp.logical_and(owner == s, there))(lambda: local_act(own))
            for side in range(2):
                to_t = t if side == 0 else 1 - t
                copy = main(slot, number, side, head, (owner, to_t))
                away = jnp.logical_and(owner != s, there) if side == 0 else there
                pl.when(away)(lambda: remote_act(copy))
                edge = halo(slot, side, head, (lax.rem(owner + seq - 1, seq), to_t))
                pl.when(jnp.logical_and(owner >= 1, there))(lambda: halo_act(edge))

    each_slot(lambda copy: copy.start(), lambda own: own.start(), lambda edge: edge.start())

    for from_head in range(2 * pairs):
        itself = jnp.logical_and(from_head % pairs == s // 2, from_head // pairs == t)
        for number, cond in ((rows, s < 8), (tail, s == 8)):
            arrived = main(0, number, 0, from_head, (s, 1 - t))
            pl.when(jnp.logical_and(cond, jnp.logical_not(itself)))(arrived.wait_recv)
        pl.when(s < 8)(halo(0, 0, from_head, (s, 1 - t)).wait_recv)

    each_slot(lambda copy: copy.wait_send(), lambda own: own.wait(), lambda edge: edge.wait_send())


def to_owners(attended, seq, rows, tail):
    dma = pltpu.SemaphoreType.DMA
    return pl.pallas_call(
        lambda *refs: owners_kernel(seq, rows, tail, *refs),
        out_shape=jax.ShapeDtypeStruct((rows + HALO, seq * attended.shape[1]), attended.dtype),
        in_specs=[pl.BlockSpec(memory_space=pl.ANY)],
        out_specs=pl.BlockSpec(memory_space=pl.ANY),
        scratch_shapes=[dma, dma((5, 2)), dma((seq,)), dma((5, 2)), dma((seq,))],
        compiler_params=pltpu.CompilerParams(collective_id=1, has_side_effects=True),
        name="to_owners",
    )(attended)


def project_kernel(mine_ref, w_ref, tokens_ref, scale_ref, real_ref, out_ref):
    total = jnp.dot(mine_ref[...], w_ref[0], preferred_element_type=jnp.float32)
    layer_out = tokens_ref[...].astype(jnp.float32) + scale_ref[...] * total
    out_ref[...] = jnp.where(real_ref[...] > 0, layer_out, 0.0).astype(out_ref.dtype)


def project(mine, out_weights, tokens, scale, real):
    count, depth = mine.shape
    blocks, _, part = out_weights.shape
    return pl.pallas_call(
        project_kernel,
        grid=(blocks,),
        out_shape=jax.ShapeDtypeStruct(tokens.shape, tokens.dtype),
        in_specs=[
            pl.BlockSpec((count, depth), lambda i: (0, 0)),
            pl.BlockSpec((1, depth, part), lambda i: (i, 0, 0)),
            pl.BlockSpec((count, part), lambda i: (0, i)),
            pl.BlockSpec((1, part), lambda i: (0, i)),
            pl.BlockSpec((count, 1), lambda i: (0, 0)),
        ],
        out_specs=pl.BlockSpec((count, part), lambda i: (0, i)),
        compiler_params=pltpu.CompilerParams(vmem_limit_bytes=56 * 1024 * 1024),
        name="project",
    )(mine, out_weights, tokens, scale, real)


def merge_kernel(pick_ref, rows_ref, out_ref):
    count, four, width = out_ref.shape
    picked = jnp.dot(pick_ref[...], rows_ref[...], preferred_element_type=jnp.float32)
    out_ref[...] = picked.reshape(count, four, width).astype(out_ref.dtype)


def merge_rows(pick, extended, count, step):
    width = extended.shape[1]
    return pl.pallas_call(
        merge_kernel,
        grid=(count // step,),
        out_shape=jax.ShapeDtypeStruct((count, 4, width), extended.dtype),
        in_specs=[
            pl.BlockSpec((4 * step, pick.shape[1]), lambda i: (i, 0)),
            pl.BlockSpec(extended.shape, lambda i: (0, 0)),
        ],
        out_specs=pl.BlockSpec((step, 4, width), lambda i: (i, 0, 0)),
        compiler_params=pltpu.CompilerParams(vmem_limit_bytes=32 * 1024 * 1024),
        name="merge_rows",
    )(pick, extended)


def head_body(tokens, ln_gain, ln_bias, w_qkv, w_out, layer_scale, grids, offsets):
    rows, width = tokens.shape
    seq = lax.axis_size("seq")
    row_count = rows * seq
    s = lax.axis_index("seq")
    tp = lax.axis_index("tp")
    core = s % 2
    tail = -(-(PAIR_ROWS - 8 * rows) // 16) * 16
    token_halo = from_behind(tokens[:HALO], "seq", -1)
    gathered, weights, columns = gather_inputs(
        tokens,
        w_qkv.reshape(w_qkv.shape[0], -1),
        w_out.reshape(-1, w_out.shape[2]),
        seq,
        tail,
    )
    out_weights = lax.all_gather(columns, "seq", axis=0, tiled=True)
    out_weights = out_weights.reshape(seq // 2, 2 * columns.shape[0], columns.shape[1])
    widened = gathered.astype(jnp.float32)
    average = jnp.mean(widened, axis=-1, keepdims=True)
    spread_sq = jnp.mean(jnp.square(widened - average), axis=-1, keepdims=True)
    normed = ((widened - average) * lax.rsqrt(spread_sq + 1e-06) * ln_gain + ln_bias).astype(
        jnp.bfloat16
    )
    size = weights.shape[1] // 3
    qkv_sums = jnp.dot(normed, weights, preferred_element_type=jnp.float32).reshape(-1, 3, size)

    slot_rows = jnp.arange(gathered.shape[0], dtype=jnp.int32)
    base_rows = (slot_rows // rows) * (2 * rows) + slot_rows % rows
    row_ids = base_rows + core * rows
    other_ids = base_rows + (1 - core) * rows
    segment, inside, is_patch, grid_row, grid_col, grid_side = layout_rows(
        row_ids, offsets, grids, row_count
    )
    turned = rotate(qkv_sums[:, :2], is_patch, grid_row, grid_col, grid_side)
    queries = turned[:, 0].astype(jnp.bfloat16)
    keys_values = jnp.concatenate([turned[:, 1], qkv_sums[:, 2]], axis=-1).astype(jnp.bfloat16)
    keys_values = jnp.where(inside[:, None], keys_values, jnp.zeros_like(keys_values))
    others = lax.ppermute(keys_values, "seq", [(i, i ^ 1) for i in range(seq)])
    all_kv = jnp.concatenate([keys_values, others], axis=0)
    other_layout = layout_rows(other_ids, offsets, grids, row_count)
    key_segment = jnp.concatenate([segment, other_layout[0]])
    key_inside = jnp.concatenate([inside, other_layout[1]])
    allowed = inside[:, None] & key_inside[None, :] & (segment[:, None] == key_segment[None, :])
    logits = jnp.dot(
        queries, all_kv[:, :size].T, preferred_element_type=jnp.float32
    ) * (1.0 / math.sqrt(size))
    masked = jnp.where(allowed, logits, -1e30)
    row_max = jnp.max(masked, axis=1, keepdims=True)
    terms = jnp.where(allowed, jnp.exp(masked - row_max), 0.0)
    total = jnp.where(inside[:, None], jnp.sum(terms, axis=1, keepdims=True), 1.0)
    soft = (terms / total).astype(jnp.bfloat16)
    attended = jnp.dot(soft, all_kv[:, size:], preferred_element_type=jnp.float32)
    attended = jnp.where(inside[:, None], attended, 0.0).astype(jnp.bfloat16)

    mine = to_owners(attended, seq, rows, tail)
    extended_tokens = jnp.concatenate([tokens, token_halo], axis=0)
    extended_ids = s * rows + jnp.arange(rows + HALO, dtype=jnp.int32)
    real = (extended_ids < offsets[-1]).astype(jnp.int32)[:, None]
    extended = project(mine, out_weights, extended_tokens, layer_scale[None, :], real)

    local_ids = jnp.arange(rows, dtype=jnp.int32)
    _, _, is_patch, grid_row, grid_col, grid_side = layout_rows(
        s * rows + local_ids, offsets, grids, row_count
    )
    is_corner = is_patch & (grid_row % 2 == 0) & (grid_col % 2 == 0)
    corner_index = jnp.stack(
        [local_ids, local_ids + 1, local_ids + grid_side, local_ids + grid_side + 1], axis=1
    )
    corner_index = jnp.where(is_corner[:, None], corner_index, -1).reshape(-1)
    pick = (
        corner_index[:, None] == jnp.arange(extended.shape[0], dtype=jnp.int32)[None, :]
    ).astype(jnp.bfloat16)
    return merge_rows(pick, extended, rows, 32)


def solution(mesh):
    placed = (
        P("seq", "tp"),
        P(),
        P(),
        P("seq", "tp", None, None),
        P("tp", None, "seq"),
        P("tp"),
        P(),
        P(),
    )
    small = mesh.shape["seq"] == 16 and mesh.shape["tp"] == 2
    return jax.shard_map(
        head_body if small else window_body,
        mesh=mesh,
        in_specs=placed,
        out_specs=P("seq", None, "tp"),
        check_vma=False,
    )
```
